128 devices in a mesh: corpus: 16 (over y, x), query: 8 (over z, core).
Axes of the slice: x: 4, y: 4, z: 4, core: 2. Of those that a mesh axis runs over, the one named last changes fastest.
Arguments:
- queries: bfloat16 [8192, 128], P('query'), may hold values from -1 to 1
- corpus: bfloat16 [131072, 128], P('corpus'), may hold values from -1 to 1
- targets: bfloat16 [131072, 128], P('corpus'), may hold values from -6 to 6
- cotangent: bfloat16 [8192, 128], P('query'), may hold values from -896 to 896
Outputs:
- grad_query: float32 [8192, 128], P('query')
- grad_corpus: float32 [131072, 128], P(('corpus', 'query'))
- grad_target: float32 [131072, 128], P(('corpus', 'query'))
The draws below stay inside these ranges and needn't reach their ends.
All inputs are finite; a program needn't handle non-finite values.
Results may differ from the reference program's by a relative error of at most 0.005.
Values may be sent and summed in bfloat16 or wider, within the bound.
No kernel may reach another device: no remote copies, remote signals or barrier semaphores. Data moves between devices by JAX's collectives and lax.ppermute only.
A program may use at most 64 MiB of HBM per device.

```python
import math
import jax
import jax.numpy as jnp
from jax import lax

E = 128
F = 128
NQ = 8192
NC = 131072


def levels(stream_key, dims, pieces, low, largest):
    def one(axis_at, shards_of):
        draws = jax.random.uniform(jax.random.fold_in(jax.random.fold_in(stream_key, 6), axis_at), (shards_of,), jnp.float32, low / len(pieces), largest / len(pieces))
        return jnp.repeat(jnp.exp(draws), dims[axis_at] // shards_of).reshape((-1,) + (1,) * (len(dims) - axis_at - 1))

    loudness = one(*pieces[0])
    for cut in pieces[1:]:
        loudness = loudness * one(*cut)
    return loudness


def gaussian(own_key, extent, scale, reach, split=(), kind=jnp.bfloat16):
    gain = levels(own_key, extent, split, -0.22, 0.18) if split else 1.0
    array = jax.random.normal(own_key, extent, jnp.float32) * scale * gain
    return jnp.minimum(jnp.maximum(array, -reach), reach).astype(kind)


def setup_inputs(seed: int = 0) -> dict:
    seeds = jax.random.split(jax.random.key(seed), 5)
    queries = jnp.clip(jax.random.uniform(seeds[0], (NQ, E), jnp.float32, -1.0, 1.0) * levels(seeds[0], (NQ, E), ((0, 8),), -0.4, 0.0), -1.0, 1.0).astype(jnp.bfloat16)
    corpus = jnp.clip(jax.random.uniform(seeds[1], (NC, E), jnp.float32, -1.0, 1.0) * levels(seeds[1], (NC, E), ((0, 16),), -0.4, 0.0), -1.0, 1.0).astype(jnp.bfloat16)
    targets = gaussian(seeds[2], (NC, F), 1.0, 6.0, ((0, 16),))
    cotangent = gaussian(seeds[3], (NQ, F), (16 + NC // 1024), 896.0, ((0, 8),))
    return dict(queries=queries, corpus=corpus, targets=targets, cotangent=cotangent)


def cross(left, right):
    return lax.dot_general(left, right, (((1,), (1,)), ((), ())), preferred_element_type=jnp.float32)

def down(left, right):
    return lax.dot_general(left, right, (((0,), (0,)), ((), ())), preferred_element_type=jnp.float32)

def reference(queries, corpus, targets, cotangent):
    beta = 4.5 / math.sqrt(E)
    block = min(1024, NC)
    count = NC // block
    ys = corpus.reshape(count, block, E)
    zs = targets.reshape(count, block, F)

    def forward(carry, item):
        total, unnorm = carry
        yb, zb = item
        half_sq = 0.5 * lax.optimization_barrier(jnp.sum(jnp.square(yb.astype(jnp.float32)), axis=1))
        kernel = jnp.exp(beta * (cross(queries, yb) - half_sq[None, :]))
        total = total + lax.optimization_barrier(jnp.sum(kernel, axis=1))
        unnorm = unnorm + jnp.dot(kernel.astype(jnp.bfloat16), zb, preferred_element_type=jnp.float32)
        return ((total, unnorm), None)
    start = (jnp.zeros((NQ,), jnp.float32), jnp.zeros((NQ, F), jnp.float32))
    (total, unnorm), _ = lax.scan(forward, start, (ys, zs))
    recip = 1.0 / total
    mixed = unnorm * recip[:, None]
    inner = lax.optimization_barrier(jnp.sum(cotangent.astype(jnp.float32) * mixed, axis=1))

    def backward(grad_acc, item):
        yb, zb = item
        half_sq = 0.5 * lax.optimization_barrier(jnp.sum(jnp.square(yb.astype(jnp.float32)), axis=1))
        prob = jnp.exp(beta * (cross(queries, yb) - half_sq[None, :])) * recip[:, None]
        score = cross(cotangent, zb)
        adjoint = (beta * prob * (score - inner[:, None])).astype(jnp.bfloat16)
        prob_b = prob.astype(jnp.bfloat16)
        grad_acc = grad_acc + jnp.dot(adjoint, yb, preferred_element_type=jnp.float32)
        colsum = lax.optimization_barrier(jnp.sum(adjoint.astype(jnp.float32), axis=0))
        grad_y = down(adjoint, queries) - colsum[:, None] * yb.astype(jnp.float32)
        grad_z = down(prob_b, cotangent)
        return (grad_acc, (grad_y, grad_z))
    grad_query, (grad_y, grad_z) = lax.scan(backward, jnp.zeros((NQ, E), jnp.float32), (ys, zs))
    return (grad_query, grad_y.reshape(NC, E), grad_z.reshape(NC, F))
```

```python
import functools
import math

import jax
import jax.numpy as jnp
from jax import lax
from jax.experimental import pallas as pl
from jax.experimental.pallas import tpu as pltpu
from jax.sharding import PartitionSpec as P

F32, BF16 = jnp.float32, jnp.bfloat16
LANES = 128
WIDE = 2 * LANES
TILE = 512
VMEM_BYTES = 56 * 1024 * 1024
NT = (((1,), (1,)), ((), ()))
NN = (((1,), (0,)), ((), ()))


def dot(left, right, dims=NN):
    return lax.dot_general(left, right, dims, preferred_element_type=F32)


def split3(value):
    high = value.astype(BF16).astype(F32)
    rest = value - high
    mid = rest.astype(BF16).astype(F32)
    return high, mid, (rest - mid).astype(BF16).astype(F32)


def columns_tail(rows, entries):
    lane = lax.broadcasted_iota(jnp.int32, (rows, LANES), 1)
    tail = jnp.zeros((rows, LANES), F32)
    for k, entry in enumerate(entries):
        tail = jnp.where(lane == k, entry, tail)
    return tail.astype(BF16)


def row_sums(array):
    return jnp.sum(array.T, axis=0, keepdims=True)


def forward_loop(scale, rows, count, qaug, yaug_ref, zaug_ref, total_ref, acc_ref):
    for i in range(rows // TILE):
        at = slice(i * TILE, (i + 1) * TILE)
        q = qaug[at, :]
        total = jnp.zeros((TILE, LANES), F32)
        acc = jnp.zeros((TILE, WIDE), F32)
        for j in range(count // TILE):
            js = slice(j * TILE, (j + 1) * TILE)
            kernel = jnp.exp2(dot(q, yaug_ref[js, :], NT) * scale)
            for u in range(TILE // LANES):
                total = total + kernel[:, u * LANES : (u + 1) * LANES]
            both = jnp.concatenate([yaug_ref[js, :LANES], zaug_ref[js, :LANES]], axis=1)
            acc = acc + dot(kernel.astype(BF16), both)
        total_ref[at, :] = total
        acc_ref[at, :] = acc


def forward_end(total_ref, acc_ref, cot_ref, caug_ref, sumk_ref):
    rows = total_ref.shape[0]
    total = total_ref[...]
    weighted = cot_ref[...].astype(F32) * acc_ref[:, LANES:]
    center = jnp.sum(weighted, axis=1, keepdims=True) / jnp.sum(total, axis=1, keepdims=True)
    caug_ref[:, :LANES] = cot_ref[...]
    caug_ref[:, LANES:] = columns_tail(rows, [-t for t in split3(center)])
    sumk_ref[...] = acc_ref[:, :LANES]
    return row_sums(total), row_sums(weighted)


def forward_a(scale, core_ref, q_ref, cot_ref, y_ref, z_ref, stats_ref, yaug_ref, zaug_ref, caug_ref, sumk_ref, qaug, total, acc):
    slices, step = y_ref.shape[0], y_ref.shape[2]
    for s in range(slices):
        at = slice(s * step, (s + 1) * step)
        y = y_ref[s, 0]
        half = 0.5 * jnp.sum(jnp.square(y.astype(F32)), axis=1, keepdims=True)
        yaug_ref[at, :LANES] = y
        yaug_ref[at, LANES:] = columns_tail(step, [*split3(half), 1.0, 1.0, 1.0])
        zaug_ref[at, :LANES] = z_ref[s, 0]
        zaug_ref[at, LANES:] = columns_tail(step, [1.0, 1.0, 1.0])
    rows = q_ref.shape[0]
    qaug[:, :LANES] = q_ref[...]
    qaug[:, LANES:] = columns_tail(rows, [-1.0, -1.0, -1.0])
    forward_loop(scale, rows, slices * step, qaug, yaug_ref, zaug_ref, total, acc)
    sums = forward_end(total, acc, cot_ref, caug_ref, sumk_ref)
    stats_ref[0:1, :] = sums[0]
    stats_ref[1:2, :] = sums[1]


def forward_b(scale, q_ref, cot_ref, yaug_ref, zaug_ref, before_ref, stats_ref, caug_ref, sumk_ref, qaug, total, acc):
    rows = q_ref.shape[0]
    qaug[:, :LANES] = q_ref[...]
    qaug[:, LANES:] = columns_tail(rows, [-1.0, -1.0, -1.0])
    forward_loop(scale, rows, yaug_ref.shape[0], qaug, yaug_ref, zaug_ref, total, acc)
    sums = forward_end(total, acc, cot_ref, caug_ref, sumk_ref)
    stats_ref[0:2, :] = before_ref[...]
    stats_ref[2:3, :] = sums[0]
    stats_ref[3:4, :] = sums[1]


def scored(scale, q_ref, caug_ref, yaug_ref, zaug_ref, sumk_ref, out_ref, qaug):
    rows, count = q_ref.shape[0], yaug_ref.shape[0]
    qaug[:, :LANES] = q_ref[...]
    qaug[:, LANES:] = columns_tail(rows, [-1.0, -1.0, -1.0])
    for i in range(rows // TILE):
        at = slice(i * TILE, (i + 1) * TILE)
        q, cot = qaug[at, :], caug_ref[at, :]
        acc = jnp.zeros((TILE, LANES), F32)
        for j in range(count // TILE):
            js = slice(j * TILE, (j + 1) * TILE)
            yaug = yaug_ref[js, :]
            kernel = jnp.exp2(dot(q, yaug, NT) * scale)
            score = dot(cot, zaug_ref[js, :], NT)
            acc = acc + dot((kernel * score).astype(BF16), yaug[:, :LANES])
        sumk = sumk_ref[at, :]
        center = -jnp.sum(cot[:, LANES:].astype(F32), axis=1, keepdims=True)
        out_ref[at, :LANES] = acc + center * sumk
        out_ref[at, LANES:] = sumk


def prepare(scale, s0, s1, s2, s3, q0, q1, c0, c1, qaug_ref, caug_ref, final_ref):
    stats = (s0[...] + s1[...]) + (s2[...] + s3[...])
    rows = q0.shape[0]
    row = lax.broadcasted_iota(jnp.int32, (LANES, rows), 0)
    for k, (q, c) in enumerate(((q0, c0), (q1, c1))):
        total = stats[2 * k : 2 * k + 1, :]
        inner = stats[2 * k + 1 : 2 * k + 2, :] / total
        lift = jnp.log2(total) * (-1.0 / scale)
        qt = jnp.where(row < 3, -1.0, jnp.zeros((LANES, rows), F32))
        ct = jnp.zeros((LANES, rows), F32)
        for n, (a, b) in enumerate(zip(split3(lift), split3(inner))):
            qt = jnp.where(row == 3 + n, a, qt)
            ct = jnp.where(row == n, -b, ct)
        at = slice(k * rows, (k + 1) * rows)
        qaug_ref[at, :LANES] = q[...]
        qaug_ref[at, LANES:] = qt.T.astype(BF16)
        caug_ref[at, :LANES] = c[...]
        caug_ref[at, LANES:] = ct.T.astype(BF16)
        final_ref[2 * k : 2 * k + 1, :] = 1.0 / total
        final_ref[2 * k + 1 : 2 * k + 2, :] = inner


def backward(scale, beta, at_ref, yaug_ref, zaug_ref, qaug_ref, caug_ref, *out_refs):
    step, rows = yaug_ref.shape[0], qaug_ref.shape[0]
    for j in range(step // TILE):
        js = slice(j * TILE, (j + 1) * TILE)
        yaug, zaug = yaug_ref[js, :], zaug_ref[js, :]
        gy = jnp.zeros((TILE, WIDE), F32)
        gz = jnp.zeros((TILE, LANES), F32)
        for i in range(rows // TILE):
            at = slice(i * TILE, (i + 1) * TILE)
            q, cot = qaug_ref[at, :], caug_ref[at, :]
            prob = jnp.exp2(dot(yaug, q, NT) * scale)
            adjoint = prob * dot(zaug, cot, NT)
            gy = gy + dot(adjoint.astype(BF16), q)
            gz = gz + dot(prob.astype(BF16), cot[:, :LANES])
        gy = beta * (gy[:, :LANES] + gy[:, LANES : LANES + 1] * yaug[:, :LANES].astype(F32))
        if len(out_refs) == 1:
            out_refs[0][js, :LANES] = gy.astype(BF16)
            out_refs[0][js, LANES:] = gz.astype(BF16)
        else:
            out_refs[0][js, :] = gy
            out_refs[1][js, :] = gz


def shape(*dims, dtype=F32):
    return jax.ShapeDtypeStruct(dims, dtype)


def vmem():
    return pl.BlockSpec(memory_space=pltpu.VMEM)


def cost(pairs, units):
    return pl.CostEstimate(flops=units * 2 * pairs * WIDE, bytes_accessed=8 << 20, transcendentals=pairs)


def call(body, name, outs, n_in, pairs, units, scratch=()):
    return pl.pallas_call(
        body,
        name=name,
        out_shape=outs,
        in_specs=[vmem()] * n_in,
        out_specs=jax.tree.map(lambda _: vmem(), outs),
        scratch_shapes=list(scratch),
        cost_estimate=cost(pairs, units),
        compiler_params=pltpu.CompilerParams(vmem_limit_bytes=VMEM_BYTES),
    )


def total_of(parts):
    return functools.reduce(lambda a, b: a + b, parts)


def body(nx, ny, nz, queries, corpus, targets, cotangent):
    rows, width = queries.shape
    owned = corpus.shape[0] // (2 * nz)
    count = nz * owned
    beta = 4.5 / math.sqrt(width)
    scale = beta * math.log2(math.e)
    column, place = lax.axis_index("corpus"), lax.axis_index("query")
    core, z = place % 2, place // 2
    x = column % nx
    swap = [(k, k ^ 1) for k in range(2 * nz)]

    def other_core(array):
        return lax.ppermute(array, "query", swap)

    def along_z(array, d):
        return lax.ppermute(array, "query", [(k, (k + 2 * d) % (2 * nz)) for k in range(2 * nz)])

    def along_x(array, d):
        return lax.ppermute(array, "corpus", [(k, k // nx * nx + (k + d) % nx) for k in range(nx * ny)])

    def along_y(array, d):
        return lax.ppermute(array, "corpus", [(k, (k + nx * d) % (nx * ny)) for k in range(nx * ny)])

    q_other = other_core(queries)
    cot_other = other_core(cotangent)
    scratch = [pltpu.VMEM((rows, WIDE), BF16), pltpu.VMEM((rows, LANES), F32), pltpu.VMEM((rows, WIDE), F32)]
    half_spec = pl.BlockSpec((nz, 1, owned, width), lambda i, c: (0, c[0], 0, 0))
    whole = lambda *dims: pl.BlockSpec(dims, lambda i, c: (0,) * len(dims))
    split = lambda a: a.reshape(nz, 2, owned, width)
    pairs = rows * count
    stats_a, yaug, zaug, caug_a, sumk_a = pl.pallas_call(
        functools.partial(forward_a, scale),
        name="forward_a",
        out_shape=[shape(2, rows), shape(count, WIDE, dtype=BF16), shape(count, WIDE, dtype=BF16), shape(rows, WIDE, dtype=BF16), shape(rows, LANES)],
        grid_spec=pltpu.PrefetchScalarGridSpec(
            num_scalar_prefetch=1,
            grid=(1,),
            in_specs=[whole(rows, width), whole(rows, width), half_spec, half_spec],
            out_specs=[whole(2, rows), whole(count, WIDE), whole(count, WIDE), whole(rows, WIDE), whole(rows, LANES)],
            scratch_shapes=scratch,
        ),
        cost_estimate=cost(pairs, 2),
        compiler_params=pltpu.CompilerParams(vmem_limit_bytes=VMEM_BYTES),
    )(core[None].astype(jnp.int32), queries, cotangent, split(corpus), split(targets))
    stats, caug_b, sumk_b = call(
        functools.partial(forward_b, scale),
        "forward_b",
        [shape(4, rows), shape(rows, WIDE, dtype=BF16), shape(rows, LANES)],
        5,
        pairs,
        2,
        scratch,
    )(q_other, cot_other, yaug, zaug, stats_a)

    stats = stats + jnp.roll(other_core(stats), 2, axis=0)
    stats = total_of([stats] + [along_x(stats, d) for d in range(1, nx)])
    arrived = [stats] + [along_y(stats, d) for d in range(1, ny)]

    query_terms = call(functools.partial(scored, scale), "scored", shape(rows, WIDE), 5, pairs, 3, scratch[:1])
    sums_b = query_terms(q_other, caug_b, yaug, zaug, sumk_b)
    sums_a = query_terms(queries, caug_a, yaug, zaug, sumk_a)

    qaug, caug, final = call(
        functools.partial(prepare, scale),
        "prepare",
        [shape(2 * rows, WIDE, dtype=BF16), shape(2 * rows, WIDE, dtype=BF16), shape(4, rows)],
        8,
        rows,
        1,
    )(*arrived, queries, q_other, cotangent, cot_other)

    sums = sums_a + other_core(sums_b)
    part = rows // nx
    quarter = lambda d: lax.dynamic_slice_in_dim(sums, (x + d) % nx * part, part, axis=0)
    mine = total_of([quarter(0)] + [along_x(quarter(d), d) for d in range(1, nx)])
    mine = total_of([mine] + [along_y(mine, d) for d in range(1, ny)])
    recip = lax.dynamic_slice_in_dim(final[0], x * part, part)[:, None]
    inner = lax.dynamic_slice_in_dim(final[1], x * part, part)[:, None]
    mine = beta * recip * (mine[:, :LANES] - inner * mine[:, LANES:])
    grad_query = jnp.zeros((rows, LANES), F32)
    for d in range(nx):
        piece = along_x(mine, d) if d else mine
        grad_query = lax.dynamic_update_slice_in_dim(grad_query, piece, (x - d) % nx * part, axis=0)

    def slice_of(d):
        at = (z + d) % nz
        piece = pl.BlockSpec((owned, WIDE), lambda i, c: (c[0], 0))
        outs = [shape(owned, WIDE, dtype=BF16)] if d else [shape(owned, LANES), shape(owned, LANES)]
        return pl.pallas_call(
            functools.partial(backward, scale, beta),
            name="backward",
            out_shape=outs,
            grid_spec=pltpu.PrefetchScalarGridSpec(
                num_scalar_prefetch=1,
                grid=(1,),
                in_specs=[piece, piece, whole(2 * rows, WIDE), whole(2 * rows, WIDE)],
                out_specs=[whole(*o.shape) for o in outs],
            ),
            cost_estimate=cost(2 * rows * owned, 4),
            compiler_params=pltpu.CompilerParams(vmem_limit_bytes=VMEM_BYTES),
        )(at[None].astype(jnp.int32), yaug, zaug, qaug, caug)

    order = sorted(range(1, nz), key=lambda d: -min(d, nz - d))
    sent = [along_z(slice_of(d)[0], d) for d in order]
    gy, gz = slice_of(0)
    for piece in sent:
        gy = gy + piece[:, :LANES].astype(F32)
        gz = gz + piece[:, LANES:].astype(F32)
    return grad_query, gy, gz


def solution(mesh):
    nx = ny = math.isqrt(mesh.shape["corpus"])
    nz = mesh.shape["query"] // 2
    placed = (P("query", None), P("corpus", None), P("corpus", None), P("query", None))
    return jax.shard_map(
        functools.partial(body, nx, ny, nz),
        mesh=mesh,
        in_specs=placed,
        out_specs=(P("query", None), P(("corpus", "query"), None), P(("corpus", "query"), None)),
        check_vma=False,
    )
```

```python
import functools
import math

import jax
import jax.numpy as jnp
from jax import lax
from jax.experimental import pallas as pl
from jax.experimental.pallas import tpu as pltpu
from jax.sharding import PartitionSpec as P

F32, BF16 = jnp.float32, jnp.bfloat16
LANES = 128
WIDE = 2 * LANES
TILE = 512
VMEM_BYTES = 8 * 1024 * 1024
NT = (((1,), (1,)), ((), ()))
NN = (((1,), (0,)), ((), ()))


def dot(left, right, dims=NN):
    return lax.dot_general(left, right, dims, preferred_element_type=F32)


def split3(value):
    high = value.astype(BF16).astype(F32)
    rest = value - high
    mid = rest.astype(BF16).astype(F32)
    return high, mid, (rest - mid).astype(BF16).astype(F32)


def columns_tail(rows, entries):
    lane = lax.broadcasted_iota(jnp.int32, (rows, LANES), 1)
    tail = jnp.zeros((rows, LANES), F32)
    for k, entry in enumerate(entries):
        tail = jnp.where(lane == k, entry, tail)
    return tail.astype(BF16)


def row_sums(array):
    return jnp.sum(array.T, axis=0, keepdims=True)


def halves(ref):
    return ref.at[:, :WIDE], ref.at[:, WIDE:]


def augment(core_ref, y_hbm, z_hbm, points_ref, y, z, sems):
    yaug_ref, zaug_ref = halves(points_ref)
    core = core_ref[0]
    copies = [pltpu.make_async_copy(h.at[:, core], v, sems.at[k]) for k, (h, v) in enumerate(((y_hbm, y), (z_hbm, z)))]
    for copy in copies:
        copy.start()
    slices, step = y.shape[:2]
    copies[0].wait()
    for s in range(slices):
        at = slice(s * step, (s + 1) * step)
        points = y[s]
        half = 0.5 * jnp.sum(jnp.square(points.astype(F32)), axis=1, keepdims=True)
        yaug_ref[at, :LANES] = points
        yaug_ref[at, LANES:] = columns_tail(step, [*split3(half), 1.0, 1.0, 1.0])
    copies[1].wait()
    for s in range(slices):
        at = slice(s * step, (s + 1) * step)
        zaug_ref[at, :LANES] = z[s]
        zaug_ref[at, LANES:] = columns_tail(step, [1.0, 1.0, 1.0])


def forward(scale, q0_ref, q1_ref, c0_ref, c1_ref, points_ref, stats_ref, kernel_ref, caug_ref, sumk_ref, qaug):
    yaug_ref, zaug_ref = halves(points_ref)
    rows, count = q0_ref.shape[0], points_ref.shape[0]
    qaug[:, LANES:] = columns_tail(2 * rows, [-1.0, -1.0, -1.0])
    for half, (q_ref, c_ref) in enumerate(((q0_ref, c0_ref), (q1_ref, c1_ref))):
        base = half * rows
        qaug[base : base + rows, :LANES] = q_ref[...]
        caug_ref[base : base + rows, :LANES] = c_ref[...]
        for i in range(rows // TILE):
            at = slice(base + i * TILE, base + (i + 1) * TILE)
            q = qaug[at, :]
            total = jnp.zeros((TILE, LANES), F32)
            acc = jnp.zeros((TILE, WIDE), F32)
            for j in range(count // TILE):
                js = slice(j * TILE, (j + 1) * TILE)
                kernel = jnp.exp2(dot(q, yaug_ref[js, :], NT) * scale)
                for u in range(TILE // LANES):
                    total = total + kernel[:, u * LANES : (u + 1) * LANES]
                rounded = kernel.astype(BF16)
                kernel_ref[at, js] = rounded
                both = jnp.concatenate([yaug_ref[js, :LANES], zaug_ref[js, :LANES]], axis=1)
                acc = acc + dot(rounded, both)
            sumk_ref[at, :] = acc[:, :LANES]
            weighted = c_ref[i * TILE : (i + 1) * TILE, :].astype(F32) * acc[:, LANES:]
            center = jnp.sum(weighted, axis=1, keepdims=True) / jnp.sum(total, axis=1, keepdims=True)
            caug_ref[at, LANES:] = columns_tail(TILE, [-t for t in split3(center)])
            cols = slice(i * TILE, (i + 1) * TILE)
            stats_ref[2 * half : 2 * half + 1, cols] = row_sums(total)
            stats_ref[2 * half + 1 : 2 * half + 2, cols] = row_sums(weighted)


def scored(half, caug_ref, points_ref, kernel_ref, _, out_ref):
    yaug_ref, zaug_ref = halves(points_ref)
    rows, count = out_ref.shape[0], points_ref.shape[0]
    for i in range(rows // TILE):
        at = slice(half * rows + i * TILE, half * rows + (i + 1) * TILE)
        cot = caug_ref[at, :]
        acc = jnp.zeros((TILE, LANES), F32)
        for j in range(count // TILE):
            js = slice(j * TILE, (j + 1) * TILE)
            score = dot(cot, zaug_ref[js, :], NT)
            weighted = kernel_ref[at, js].astype(F32) * score
            acc = acc + dot(weighted.astype(BF16), yaug_ref[js, :LANES])
        out_ref[i * TILE : (i + 1) * TILE, :] = acc


def prepare(scale, beta, s0, s1, s2, s3, q0, q1, caug_f, sumk, sums0, sums1, both_ref, g0, g1):
    qaug_ref, caug_ref = halves(both_ref)
    stats = (s0[...] + s2[...]) + (s1[...] + s3[...])
    rows = q0.shape[0]
    row = lax.broadcasted_iota(jnp.int32, (LANES, rows), 0)
    for k, (q, sums, g) in enumerate(((q0, sums0, g0), (q1, sums1, g1))):
        total = stats[2 * k : 2 * k + 1, :]
        recip = 1.0 / total
        inner = stats[2 * k + 1 : 2 * k + 2, :] * recip
        lift = jnp.log2(total) * (-1.0 / scale)
        qt = jnp.where(row < 3, -1.0, jnp.zeros((LANES, rows), F32))
        ct = jnp.where(row == 3, recip * beta, jnp.zeros((LANES, rows), F32))
        for n, (a, b) in enumerate(zip(split3(lift), split3(inner))):
            qt = jnp.where(row == 3 + n, a, qt)
            ct = jnp.where(row == n, -b, ct)
        at = slice(k * rows, (k + 1) * rows)
        ct = ct.T
        lane = lax.broadcasted_iota(jnp.int32, (rows, LANES), 1)
        qaug_ref[at, :LANES] = q[...]
        qaug_ref[at, LANES:] = qt.T.astype(BF16)
        caug_ref[at, :LANES] = caug_f[at, :LANES]
        caug_ref[at, LANES:] = jnp.where(lane < 3, ct, 0.0).astype(BF16)
        center = -jnp.sum(caug_f[at, LANES:].astype(F32), axis=1, keepdims=True)
        shift = jnp.sum(jnp.where(lane < 3, ct, 0.0), axis=1, keepdims=True) + center
        g[...] = (ct[:, 3:4] * (sums[...] + shift * sumk[at, :])).astype(BF16)


def backward(scale, beta, at_ref, points_ref, both_ref, _, *out_refs):
    (yaug_ref, zaug_ref), (qaug_ref, caug_ref) = halves(points_ref), halves(both_ref)
    step, rows = points_ref.shape[0], both_ref.shape[0]
    for j in range(step // TILE):
        js = slice(j * TILE, (j + 1) * TILE)
        yaug, zaug = yaug_ref[js, :], zaug_ref[js, :]
        gy = jnp.zeros((TILE, WIDE), F32)
        gz = jnp.zeros((TILE, LANES), F32)
        for i in range(rows // TILE):
            at = slice(i * TILE, (i + 1) * TILE)
            q, cot = qaug_ref[at, :], caug_ref[at, :]
            prob = jnp.exp2(dot(yaug, q, NT) * scale)
            adjoint = prob * dot(zaug, cot, NT)
            gy = gy + dot(adjoint.astype(BF16), q)
            gz = gz + dot(prob.astype(BF16), cot[:, :LANES])
        gy = beta * (gy[:, :LANES] + gy[:, LANES : LANES + 1] * yaug[:, :LANES].astype(F32))
        if len(out_refs) == 1:
            out_refs[0][js, :LANES] = gy.astype(BF16)
            out_refs[0][js, LANES:] = gz.astype(BF16)
        else:
            out_refs[0][js, :] = gy
            out_refs[1][js, :] = gz


def shape(*dims, dtype=F32):
    return jax.ShapeDtypeStruct(dims, dtype)


def kept(*dims, dtype=F32):
    return pltpu.VMEM(dims, dtype)


def vmem():
    return pl.BlockSpec(memory_space=pltpu.VMEM)


def cost(pairs, units):
    return pl.CostEstimate(flops=units * 2 * pairs * WIDE, bytes_accessed=1 << 16, transcendentals=0)


def call(body, name, outs, n_in, pairs, units, scratch=(), unread=0):
    return pl.pallas_call(
        body,
        name=name,
        out_shape=outs,
        in_specs=[vmem()] * n_in + [pl.BlockSpec(memory_space=pl.ANY)] * unread,
        out_specs=jax.tree.map(lambda _: vmem(), outs),
        scratch_shapes=list(scratch),
        cost_estimate=cost(pairs, units),
        compiler_params=pltpu.CompilerParams(vmem_limit_bytes=VMEM_BYTES),
    )


def in_vmem(array):
    return pltpu.with_memory_space_constraint(array, pltpu.VMEM)


def ring_sum(array, along, n):
    parts = [array] + [along(array, d) for d in range(1, n)]
    return (parts[0].astype(F32) + parts[2].astype(F32)) + (parts[1].astype(F32) + parts[3].astype(F32))


def body(nx, ny, nz, queries, corpus, targets, cotangent):
    rows, width = queries.shape
    owned = corpus.shape[0] // (2 * nz)
    count = nz * owned
    beta = 4.5 / math.sqrt(width)
    scale = beta * math.log2(math.e)
    place = lax.axis_index("query")
    core, z = place % 2, place // 2
    swap = [(k, k ^ 1) for k in range(2 * nz)]

    def other_core(array):
        return lax.ppermute(array, "query", swap)

    def along_z(array, d):
        return lax.ppermute(array, "query", [(k, (k + 2 * d) % (2 * nz)) for k in range(2 * nz)])

    def along_x(array, d):
        return lax.ppermute(array, "corpus", [(k, k // nx * nx + (k + d) % nx) for k in range(nx * ny)])

    def along_y(array, d):
        return lax.ppermute(array, "corpus", [(k, (k + nx * d) % (nx * ny)) for k in range(nx * ny)])

    q_other = other_core(queries)
    cot_other = other_core(cotangent)
    pairs = rows * count
    whole = lambda *dims: pl.BlockSpec(dims, lambda i, c: (0,) * len(dims))
    in_hbm = pl.BlockSpec(memory_space=pltpu.HBM)
    split = lambda a: a.reshape(nz, 2, owned, width)
    points = pl.pallas_call(
        augment,
        name="augment",
        out_shape=kept(count, 2 * WIDE, dtype=BF16),
        in_specs=[pl.BlockSpec(memory_space=pltpu.SMEM), in_hbm, in_hbm],
        out_specs=vmem(),
        scratch_shapes=[pltpu.VMEM((nz, owned, width), BF16)] * 2 + [pltpu.SemaphoreType.DMA((2,))],
        compiler_params=pltpu.CompilerParams(vmem_limit_bytes=VMEM_BYTES),
    )(core[None].astype(jnp.int32), *(pltpu.with_memory_space_constraint(split(a), pltpu.HBM) for a in (corpus, targets)))
    stats, kernel, caug_f, sumk = call(
        functools.partial(forward, scale),
        "forward",
        [shape(4, rows), kept(2 * rows, count, dtype=BF16), kept(2 * rows, WIDE, dtype=BF16), kept(2 * rows, LANES)],
        5,
        2 * pairs,
        2,
        [pltpu.VMEM((2 * rows, WIDE), BF16)],
    )(queries, q_other, cotangent, cot_other, in_vmem(points))

    points, kernel, caug_f, sumk = (in_vmem(a) for a in (points, kernel, caug_f, sumk))
    query_terms = lambda half, after: call(functools.partial(scored, half), "scored", shape(rows, LANES), 3, pairs, 2, unread=1)(
        caug_f, points, kernel, after
    )
    stats = stats + jnp.roll(other_core(stats), 2, axis=0)
    sums1 = query_terms(1, stats)
    stats = ring_sum(stats, along_x, nx)
    sums0 = query_terms(0, stats)
    arrived = [stats] + [along_y(stats, d) for d in range(1, ny)]
    both, g0, g1 = call(
        functools.partial(prepare, scale, beta),
        "prepare",
        [kept(2 * rows, 2 * WIDE, dtype=BF16), shape(rows, LANES, dtype=BF16), shape(rows, LANES, dtype=BF16)],
        10,
        rows,
        1,
    )(*arrived, queries, q_other, caug_f, sumk, sums0, sums1)
    both = in_vmem(both)

    g = (g0.astype(F32) + other_core(g1).astype(F32)).astype(BF16)
    gx = ring_sum(g, along_x, nx).astype(BF16)
    grad_query = ring_sum(gx, along_y, ny)

    def slice_of(d, after):
        at = (z + d) % nz
        piece = pl.BlockSpec((owned, 2 * WIDE), lambda i, c: (c[0], 0))
        outs = [shape(owned, WIDE, dtype=BF16)] if d else [shape(owned, LANES), shape(owned, LANES)]
        return pl.pallas_call(
            functools.partial(backward, scale, beta),
            name="backward",
            out_shape=outs,
            grid_spec=pltpu.PrefetchScalarGridSpec(
                num_scalar_prefetch=1,
                grid=(1,),
                in_specs=[piece, whole(2 * rows, 2 * WIDE), pl.BlockSpec(memory_space=pl.ANY)],
                out_specs=[whole(*o.shape) for o in outs],
            ),
            cost_estimate=cost(1, 4),
            compiler_params=pltpu.CompilerParams(vmem_limit_bytes=VMEM_BYTES),
        )(at[None].astype(jnp.int32), points, both, after)

    order = sorted(range(1, nz), key=lambda d: -min(d, nz - d))
    sent = [along_z(slice_of(d, after)[0], d) for d, after in zip(order, (g0, g, g))]
    own = slice_of(0, gx)
    for piece in sent:
        own = lax.optimization_barrier((own[0] + piece[:, :LANES].astype(F32), own[1] + piece[:, LANES:].astype(F32)))
    gy, gz = own
    return grad_query, gy, gz


def solution(mesh):
    nx = ny = math.isqrt(mesh.shape["corpus"])
    nz = mesh.shape["query"] // 2
    placed = (P("query", None), P("corpus", None), P("corpus", None), P("query", None))
    return jax.shard_map(
        functools.partial(body, nx, ny, nz),
        mesh=mesh,
        in_specs=placed,
        out_specs=(P("query", None), P(("corpus", "query"), None), P(("corpus", "query"), None)),
        check_vma=False,
    )
```

```python
import functools
import math

import jax
import jax.numpy as jnp
from jax import lax
from jax.experimental import pallas as pl
from jax.experimental.pallas import tpu as pltpu
from jax.sharding import PartitionSpec as P

F32, BF16 = jnp.float32, jnp.bfloat16
LANES = 128
WIDE = 2 * LANES
TILE = 512
VMEM_BYTES = 8 * 1024 * 1024
NT = (((1,), (1,)), ((), ()))
NN = (((1,), (0,)), ((), ()))


def dot(left, right, dims=NN):
    return lax.dot_general(left, right, dims, preferred_element_type=F32)


def split3(value):
    high = value.astype(BF16).astype(F32)
    rest = value - high
    mid = rest.astype(BF16).astype(F32)
    return high, mid, (rest - mid).astype(BF16).astype(F32)


def columns_tail(rows, entries):
    lane = lax.broadcasted_iota(jnp.int32, (rows, LANES), 1)
    tail = jnp.zeros((rows, LANES), F32)
    for k, entry in enumerate(entries):
        tail = jnp.where(lane == k, entry, tail)
    return tail.astype(BF16)


def row_sums(array):
    return jnp.sum(array.T, axis=0, keepdims=True)


def halves(ref):
    return ref.at[:, :WIDE], ref.at[:, WIDE:]


def augment(place_ref, y_hbm, z_hbm, points_ref, y, z, sems):
    yaug_ref, zaug_ref = halves(points_ref)
    core = lax.rem(place_ref[0], 2)
    copies = [pltpu.make_async_copy(h.at[:, core], v, sems.at[k]) for k, (h, v) in enumerate(((y_hbm, y), (z_hbm, z)))]
    for copy in copies:
        copy.start()
    slices, step = y.shape[:2]
    copies[0].wait()
    for s in range(slices):
        at = slice(s * step, (s + 1) * step)
        points = y[s]
        half = 0.5 * jnp.sum(jnp.square(points.astype(F32)), axis=1, keepdims=True)
        yaug_ref[at, :LANES] = points
        yaug_ref[at, LANES:] = columns_tail(step, [*split3(half), 1.0, 1.0, 1.0])
    copies[1].wait()
    for s in range(slices):
        at = slice(s * step, (s + 1) * step)
        zaug_ref[at, :LANES] = z[s]
        zaug_ref[at, LANES:] = columns_tail(step, [1.0, 1.0, 1.0])


def forward(scale, q0_ref, q1_ref, c0_ref, c1_ref, points_ref, stats_ref, kernel_ref, caug_ref, sumk_ref, qaug):
    yaug_ref, zaug_ref = halves(points_ref)
    rows, count = q0_ref.shape[0], points_ref.shape[0]
    qaug[:, LANES:] = columns_tail(2 * rows, [-1.0, -1.0, -1.0])
    for half, (q_ref, c_ref) in enumerate(((q0_ref, c0_ref), (q1_ref, c1_ref))):
        base = half * rows
        qaug[base : base + rows, :LANES] = q_ref[...]
        caug_ref[base : base + rows, :LANES] = c_ref[...]
        for i in range(rows // TILE):
            at = slice(base + i * TILE, base + (i + 1) * TILE)
            q = qaug[at, :]
            total = jnp.zeros((TILE, LANES), F32)
            acc = jnp.zeros((TILE, WIDE), F32)
            for j in range(count // TILE):
                js = slice(j * TILE, (j + 1) * TILE)
                kernel = jnp.exp2(dot(q, yaug_ref[js, :], NT) * scale)
                for u in range(TILE // LANES):
                    total = total + kernel[:, u * LANES : (u + 1) * LANES]
                rounded = kernel.astype(BF16)
                kernel_ref[at, js] = rounded
                both = jnp.concatenate([yaug_ref[js, :LANES], zaug_ref[js, :LANES]], axis=1)
                acc = acc + dot(rounded, both)
            sumk_ref[at, :] = acc[:, :LANES]
            weighted = c_ref[i * TILE : (i + 1) * TILE, :].astype(F32) * acc[:, LANES:]
            center = jnp.sum(weighted, axis=1, keepdims=True) / jnp.sum(total, axis=1, keepdims=True)
            caug_ref[at, LANES:] = columns_tail(TILE, [-t for t in split3(center)])
            cols = slice(i * TILE, (i + 1) * TILE)
            stats_ref[2 * half : 2 * half + 1, cols] = row_sums(total)
            stats_ref[2 * half + 1 : 2 * half + 2, cols] = row_sums(weighted)


def scored(half, caug_ref, points_ref, kernel_ref, _, out_ref):
    yaug_ref, zaug_ref = halves(points_ref)
    rows, count = out_ref.shape[0], points_ref.shape[0]
    for i in range(rows // TILE):
        at = slice(half * rows + i * TILE, half * rows + (i + 1) * TILE)
        cot = caug_ref[at, :]
        acc = jnp.zeros((TILE, LANES), F32)
        for j in range(count // TILE):
            js = slice(j * TILE, (j + 1) * TILE)
            score = dot(cot, zaug_ref[js, :], NT)
            weighted = kernel_ref[at, js].astype(F32) * score
            acc = acc + dot(weighted.astype(BF16), yaug_ref[js, :LANES])
        out_ref[i * TILE : (i + 1) * TILE, :] = acc


def prepare(scale, beta, s0, s1, s2, s3, q0, q1, caug_f, sumk, sums0, sums1, both_ref, g0, g1):
    qaug_ref, caug_ref = halves(both_ref)
    stats = (s0[...] + s2[...]) + (s1[...] + s3[...])
    rows = q0.shape[0]
    row = lax.broadcasted_iota(jnp.int32, (LANES, rows), 0)
    for k, (q, sums, g) in enumerate(((q0, sums0, g0), (q1, sums1, g1))):
        total = stats[2 * k : 2 * k + 1, :]
        recip = 1.0 / total
        inner = stats[2 * k + 1 : 2 * k + 2, :] * recip
        lift = jnp.log2(total) * (-1.0 / scale)
        qt = jnp.where(row < 3, -1.0, jnp.zeros((LANES, rows), F32))
        ct = jnp.where(row == 3, recip * beta, jnp.zeros((LANES, rows), F32))
        for n, (a, b) in enumerate(zip(split3(lift), split3(inner))):
            qt = jnp.where(row == 3 + n, a, qt)
            ct = jnp.where(row == n, -b, ct)
        at = slice(k * rows, (k + 1) * rows)
        ct = ct.T
        lane = lax.broadcasted_iota(jnp.int32, (rows, LANES), 1)
        qaug_ref[at, :LANES] = q[...]
        qaug_ref[at, LANES:] = qt.T.astype(BF16)
        caug_ref[at, :LANES] = caug_f[at, :LANES]
        caug_ref[at, LANES:] = jnp.where(lane < 3, ct, 0.0).astype(BF16)
        center = -jnp.sum(caug_f[at, LANES:].astype(F32), axis=1, keepdims=True)
        shift = jnp.sum(jnp.where(lane < 3, ct, 0.0), axis=1, keepdims=True) + center
        g[...] = ct[:, 3:4] * (sums[...] + shift * sumk[at, :])


def backward(scale, beta, at_ref, points_ref, both_ref, _, *out_refs):
    (yaug_ref, zaug_ref), (qaug_ref, caug_ref) = halves(points_ref), halves(both_ref)
    step, rows = points_ref.shape[0], both_ref.shape[0]
    for j in range(step // TILE):
        js = slice(j * TILE, (j + 1) * TILE)
        yaug, zaug = yaug_ref[js, :], zaug_ref[js, :]
        gy = jnp.zeros((TILE, WIDE), F32)
        gz = jnp.zeros((TILE, LANES), F32)
        for i in range(rows // TILE):
            at = slice(i * TILE, (i + 1) * TILE)
            q, cot = qaug_ref[at, :], caug_ref[at, :]
            prob = jnp.exp2(dot(yaug, q, NT) * scale)
            adjoint = prob * dot(zaug, cot, NT)
            gy = gy + dot(adjoint.astype(BF16), q)
            gz = gz + dot(prob.astype(BF16), cot[:, :LANES])
        gy = beta * (gy[:, :LANES] + gy[:, LANES : LANES + 1] * yaug[:, :LANES].astype(F32))
        if len(out_refs) == 1:
            out_refs[0][js, :LANES] = gy.astype(BF16)
            out_refs[0][js, LANES:] = gz.astype(BF16)
        else:
            out_refs[0][js, :] = gy
            out_refs[1][js, :] = gz


def shape(*dims, dtype=F32):
    return jax.ShapeDtypeStruct(dims, dtype)


def kept(*dims, dtype=F32):
    return pltpu.VMEM(dims, dtype)


def vmem():
    return pl.BlockSpec(memory_space=pltpu.VMEM)


def cost(pairs, units):
    return pl.CostEstimate(flops=units * 2 * pairs * WIDE, bytes_accessed=1 << 16, transcendentals=0)


def call(body, name, outs, n_in, pairs, units, scratch=(), unread=0):
    return pl.pallas_call(
        body,
        name=name,
        out_shape=outs,
        in_specs=[vmem()] * n_in + [pl.BlockSpec(memory_space=pl.ANY)] * unread,
        out_specs=jax.tree.map(lambda _: vmem(), outs),
        scratch_shapes=list(scratch),
        cost_estimate=cost(pairs, units),
        compiler_params=pltpu.CompilerParams(vmem_limit_bytes=VMEM_BYTES),
    )


def in_vmem(array):
    return pltpu.with_memory_space_constraint(array, pltpu.VMEM)


def ring_sum(array, along, n):
    parts = [array] + [along(array, d) for d in range(1, n)]
    return (parts[0].astype(F32) + parts[2].astype(F32)) + (parts[1].astype(F32) + parts[3].astype(F32))


def body(nx, ny, nz, queries, corpus, targets, cotangent):
    rows, width = queries.shape
    owned = corpus.shape[0] // (2 * nz)
    count = nz * owned
    beta = 4.5 / math.sqrt(width)
    scale = beta * math.log2(math.e)
    place = lax.axis_index("query").astype(jnp.int32)[None]
    swap = [(k, k ^ 1) for k in range(2 * nz)]

    def other_core(array):
        return lax.ppermute(array, "query", swap)

    def along_z(array, d):
        return lax.ppermute(array, "query", [(k, (k + 2 * d) % (2 * nz)) for k in range(2 * nz)])

    def along_x(array, d):
        return lax.ppermute(array, "corpus", [(k, k // nx * nx + (k + d) % nx) for k in range(nx * ny)])

    def along_y(array, d):
        return lax.ppermute(array, "corpus", [(k, (k + nx * d) % (nx * ny)) for k in range(nx * ny)])

    q_other = other_core(queries)
    cot_other = other_core(cotangent)
    pairs = rows * count
    whole = lambda *dims: pl.BlockSpec(dims, lambda i, c: (0,) * len(dims))
    in_hbm = pl.BlockSpec(memory_space=pltpu.HBM)
    split = lambda a: a.reshape(nz, 2, owned, width)
    points = pl.pallas_call(
        augment,
        name="augment",
        out_shape=kept(count, 2 * WIDE, dtype=BF16),
        in_specs=[pl.BlockSpec(memory_space=pltpu.SMEM), in_hbm, in_hbm],
        out_specs=vmem(),
        scratch_shapes=[pltpu.VMEM((nz, owned, width), BF16)] * 2 + [pltpu.SemaphoreType.DMA((2,))],
        compiler_params=pltpu.CompilerParams(vmem_limit_bytes=VMEM_BYTES),
    )(place, *(pltpu.with_memory_space_constraint(split(a), pltpu.HBM) for a in (corpus, targets)))
    stats, kernel, caug_f, sumk = call(
        functools.partial(forward, scale),
        "forward",
        [shape(4, rows), kept(2 * rows, count, dtype=BF16), kept(2 * rows, WIDE, dtype=BF16), kept(2 * rows, LANES)],
        5,
        2 * pairs,
        2,
        [pltpu.VMEM((2 * rows, WIDE), BF16)],
    )(queries, q_other, cotangent, cot_other, in_vmem(points))

    points, kernel, caug_f, sumk = (in_vmem(a) for a in (points, kernel, caug_f, sumk))
    query_terms = lambda half, after: call(functools.partial(scored, half), "scored", shape(rows, LANES), 3, pairs, 2, unread=1)(
        caug_f, points, kernel, after
    )
    stats = stats + jnp.roll(other_core(stats), 2, axis=0)
    sums1 = query_terms(1, stats)
    stats = ring_sum(stats, along_x, nx)
    sums0 = query_terms(0, stats)
    arrived = [stats] + [along_y(stats, d) for d in range(1, ny)]
    both, g0, g1 = call(
        functools.partial(prepare, scale, beta),
        "prepare",
        [kept(2 * rows, 2 * WIDE, dtype=BF16), kept(rows, LANES), kept(rows, LANES)],
        10,
        rows,
        1,
    )(*arrived, queries, q_other, caug_f, sumk, sums0, sums1)
    both = in_vmem(both)

    g = (g0 + other_core(g1)).astype(BF16)
    gx = ring_sum(g, along_x, nx).astype(BF16)
    grad_query = ring_sum(gx, along_y, ny)

    def slice_of(d, after):
        piece = pl.BlockSpec((owned, 2 * WIDE), lambda i, c: (lax.rem(lax.div(c[0], 2) + d, nz), 0))
        outs = [shape(owned, WIDE, dtype=BF16)] if d else [shape(owned, LANES), shape(owned, LANES)]
        return pl.pallas_call(
            functools.partial(backward, scale, beta),
            name="backward",
            out_shape=outs,
            grid_spec=pltpu.PrefetchScalarGridSpec(
                num_scalar_prefetch=1,
                grid=(1,),
                in_specs=[piece, whole(2 * rows, 2 * WIDE), pl.BlockSpec(memory_space=pl.ANY)],
                out_specs=[whole(*o.shape) for o in outs],
            ),
            cost_estimate=cost(1, 4),
            compiler_params=pltpu.CompilerParams(vmem_limit_bytes=VMEM_BYTES),
        )(place, points, both, after)

    order = sorted(range(1, nz), key=lambda d: -min(d, nz - d))
    sent = [along_z(slice_of(d, after)[0], d) for d, after in zip(order, (g0, g, g))]
    own = slice_of(0, gx)
    for piece in sent:
        own = lax.optimization_barrier((own[0] + piece[:, :LANES].astype(F32), own[1] + piece[:, LANES:].astype(F32)))
    gy, gz = own
    return grad_query, gy, gz


def solution(mesh):
    nx = ny = math.isqrt(mesh.shape["corpus"])
    nz = mesh.shape["query"] // 2
    placed = (P("query", None), P("corpus", None), P("corpus", None), P("query", None))
    return jax.shard_map(
        functools.partial(body, nx, ny, nz),
        mesh=mesh,
        in_specs=placed,
        out_specs=(P("query", None), P(("corpus", "query"), None), P(("corpus", "query"), None)),
        check_vma=False,
    )
```

```python
import functools
import math

import jax
import jax.numpy as jnp
from jax import lax
from jax.experimental import pallas as pl
from jax.experimental.pallas import tpu as pltpu
from jax.sharding import PartitionSpec as P

F32, BF16 = jnp.float32, jnp.bfloat16
LANES = 128
WIDE = 2 * LANES
TILE = 512
SHORT, LONG = 256, 1024
VMEM_BYTES = 8 * 1024 * 1024
NT = (((1,), (1,)), ((), ()))
NN = (((1,), (0,)), ((), ()))


def dot(left, right, dims=NN):
    return lax.dot_general(left, right, dims, preferred_element_type=F32)


def split3(value):
    high = value.astype(BF16).astype(F32)
    rest = value - high
    mid = rest.astype(BF16).astype(F32)
    return high, mid, (rest - mid).astype(BF16).astype(F32)


def columns_tail(rows, entries):
    lane = lax.broadcasted_iota(jnp.int32, (rows, LANES), 1)
    tail = jnp.zeros((rows, LANES), F32)
    for k, entry in enumerate(entries):
        tail = jnp.where(lane == k, entry, tail)
    return tail.astype(BF16)


def row_sums(array):
    return jnp.sum(array.T, axis=0, keepdims=True)


def halves(ref):
    return ref.at[:, :WIDE], ref.at[:, WIDE:]


def augment(place_ref, y_hbm, z_hbm, points_ref, y, z, sems):
    yaug_ref, zaug_ref = halves(points_ref)
    core = lax.rem(place_ref[0], 2)
    slices, step = y.shape[:2]
    copies = [[pltpu.make_async_copy(h.at[s, core], v.at[s], sems.at[k, s]) for k, (h, v) in enumerate(((y_hbm, y), (z_hbm, z)))] for s in range(slices)]
    for pair in copies:
        for copy in pair:
            copy.start()
    zaug_ref[:, LANES:] = columns_tail(slices * step, [1.0, 1.0, 1.0])
    for s in range(slices):
        at = slice(s * step, (s + 1) * step)
        copies[s][0].wait()
        points = y[s]
        half = 0.5 * jnp.sum(jnp.square(points.astype(F32)), axis=1, keepdims=True)
        yaug_ref[at, :LANES] = points
        yaug_ref[at, LANES:] = columns_tail(step, [*split3(half), 1.0, 1.0, 1.0])
    for s in range(slices):
        copies[s][1].wait()
        zaug_ref[s * step : (s + 1) * step, :LANES] = z[s]


def forward(scale, q0_ref, q1_ref, c0_ref, c1_ref, points_ref, stats_ref, kernel_ref, caug_ref, sumk_ref, qaug):
    yaug_ref, zaug_ref = halves(points_ref)
    rows, count = q0_ref.shape[0], points_ref.shape[0]
    qaug[:, LANES:] = columns_tail(2 * rows, [-1.0, -1.0, -1.0])
    for half, (q_ref, c_ref) in enumerate(((q0_ref, c0_ref), (q1_ref, c1_ref))):
        base = half * rows
        qaug[base : base + rows, :LANES] = q_ref[...]
        caug_ref[base : base + rows, :LANES] = c_ref[...]
        for i in range(rows // SHORT):
            at = slice(base + i * SHORT, base + (i + 1) * SHORT)
            q = qaug[at, :]
            total = jnp.zeros((SHORT, LANES), F32)
            acc = jnp.zeros((SHORT, WIDE), F32)
            for j in range(count // LONG):
                js = slice(j * LONG, (j + 1) * LONG)
                kernel = jnp.exp2(dot(q, yaug_ref[js, :], NT) * scale)
                for u in range(LONG // LANES):
                    total = total + kernel[:, u * LANES : (u + 1) * LANES]
                rounded = kernel.astype(BF16)
                kernel_ref[at, js] = rounded
                both = jnp.concatenate([yaug_ref[js, :LANES], zaug_ref[js, :LANES]], axis=1)
                acc = acc + dot(rounded, both)
            sumk_ref[at, :] = acc[:, :LANES]
            weighted = c_ref[i * SHORT : (i + 1) * SHORT, :].astype(F32) * acc[:, LANES:]
            center = jnp.sum(weighted, axis=1, keepdims=True) / jnp.sum(total, axis=1, keepdims=True)
            caug_ref[at, LANES:] = columns_tail(SHORT, [-t for t in split3(center)])
            cols = slice(i * SHORT, (i + 1) * SHORT)
            stats_ref[2 * half : 2 * half + 1, cols] = row_sums(total)
            stats_ref[2 * half + 1 : 2 * half + 2, cols] = row_sums(weighted)


def scored(half, caug_ref, points_ref, kernel_ref, _, out_ref):
    yaug_ref, zaug_ref = halves(points_ref)
    rows, count = out_ref.shape[0], points_ref.shape[0]
    for i in range(rows // SHORT):
        at = slice(half * rows + i * SHORT, half * rows + (i + 1) * SHORT)
        cot = caug_ref[at, :]
        acc = jnp.zeros((SHORT, LANES), F32)
        for j in range(count // LONG):
            js = slice(j * LONG, (j + 1) * LONG)
            score = dot(cot, zaug_ref[js, :], NT)
            weighted = kernel_ref[at, js].astype(F32) * score
            acc = acc + dot(weighted.astype(BF16), yaug_ref[js, :LANES])
        out_ref[i * SHORT : (i + 1) * SHORT, :] = acc


def prepare(scale, beta, s0, s1, s2, s3, q0, q1, caug_f, sumk, sums0, sums1, both_ref, g0, g1):
    qaug_ref, caug_ref = halves(both_ref)
    stats = (s0[...] + s2[...]) + (s1[...] + s3[...])
    rows = q0.shape[0]
    row = lax.broadcasted_iota(jnp.int32, (LANES, rows), 0)
    for k, (q, sums, g) in enumerate(((q0, sums0, g0), (q1, sums1, g1))):
        total = stats[2 * k : 2 * k + 1, :]
        recip = 1.0 / total
        inner = stats[2 * k + 1 : 2 * k + 2, :] * recip
        lift = jnp.log2(total) * (-1.0 / scale)
        qt = jnp.where(row < 3, -1.0, jnp.zeros((LANES, rows), F32))
        ct = jnp.where(row == 3, recip * beta, jnp.zeros((LANES, rows), F32))
        for n, (a, b) in enumerate(zip(split3(lift), split3(inner))):
            qt = jnp.where(row == 3 + n, a, qt)
            ct = jnp.where(row == n, -b, ct)
        at = slice(k * rows, (k + 1) * rows)
        ct = ct.T
        lane = lax.broadcasted_iota(jnp.int32, (rows, LANES), 1)
        qaug_ref[at, :LANES] = q[...]
        qaug_ref[at, LANES:] = qt.T.astype(BF16)
        caug_ref[at, :LANES] = caug_f[at, :LANES]
        caug_ref[at, LANES:] = jnp.where(lane < 3, ct, 0.0).astype(BF16)
        center = -jnp.sum(caug_f[at, LANES:].astype(F32), axis=1, keepdims=True)
        shift = jnp.sum(jnp.where(lane < 3, ct, 0.0), axis=1, keepdims=True) + center
        g[...] = ct[:, 3:4] * (sums[...] + shift * sumk[at, :])


def backward(scale, beta, at_ref, points_ref, both_ref, _, *out_refs):
    (yaug_ref, zaug_ref), (qaug_ref, caug_ref) = halves(points_ref), halves(both_ref)
    step, rows = points_ref.shape[0], both_ref.shape[0]
    for j in range(step // TILE):
        js = slice(j * TILE, (j + 1) * TILE)
        yaug, zaug = yaug_ref[js, :], zaug_ref[js, :]
        gy = jnp.zeros((TILE, WIDE), F32)
        gz = jnp.zeros((TILE, LANES), F32)
        for i in range(rows // TILE):
            at = slice(i * TILE, (i + 1) * TILE)
            q, cot = qaug_ref[at, :], caug_ref[at, :]
            prob = jnp.exp2(dot(yaug, q, NT) * scale)
            adjoint = prob * dot(zaug, cot, NT)
            gy = gy + dot(adjoint.astype(BF16), q)
            gz = gz + dot(prob.astype(BF16), cot[:, :LANES])
        gy = beta * (gy[:, :LANES] + gy[:, LANES : LANES + 1] * yaug[:, :LANES].astype(F32))
        if len(out_refs) == 1:
            out_refs[0][js, :LANES] = gy.astype(BF16)
            out_refs[0][js, LANES:] = gz.astype(BF16)
        else:
            out_refs[0][js, :] = gy
            out_refs[1][js, :] = gz


def shape(*dims, dtype=F32):
    return jax.ShapeDtypeStruct(dims, dtype)


def kept(*dims, dtype=F32):
    return pltpu.VMEM(dims, dtype)


def vmem():
    return pl.BlockSpec(memory_space=pltpu.VMEM)


def cost(pairs, units):
    return pl.CostEstimate(flops=units * 2 * pairs * WIDE, bytes_accessed=1 << 16, transcendentals=0)


def call(body, name, outs, n_in, pairs, units, scratch=(), unread=0):
    return pl.pallas_call(
        body,
        name=name,
        out_shape=outs,
        in_specs=[vmem()] * n_in + [pl.BlockSpec(memory_space=pl.ANY)] * unread,
        out_specs=jax.tree.map(lambda _: vmem(), outs),
        scratch_shapes=list(scratch),
        cost_estimate=cost(pairs, units),
        compiler_params=pltpu.CompilerParams(vmem_limit_bytes=VMEM_BYTES),
    )


def in_vmem(array):
    return pltpu.with_memory_space_constraint(array, pltpu.VMEM)


def ring_sum(array, along, n):
    parts = [array] + [along(array, d) for d in range(1, n)]
    return (parts[0].astype(F32) + parts[2].astype(F32)) + (parts[1].astype(F32) + parts[3].astype(F32))


def body(nx, ny, nz, queries, corpus, targets, cotangent):
    rows, width = queries.shape
    owned = corpus.shape[0] // (2 * nz)
    count = nz * owned
    beta = 4.5 / math.sqrt(width)
    scale = beta * math.log2(math.e)
    place = lax.axis_index("query").astype(jnp.int32)[None]
    swap = [(k, k ^ 1) for k in range(2 * nz)]

    def other_core(array):
        return lax.ppermute(array, "query", swap)

    def along_z(array, d):
        return lax.ppermute(array, "query", [(k, (k + 2 * d) % (2 * nz)) for k in range(2 * nz)])

    def along_x(array, d):
        return lax.ppermute(array, "corpus", [(k, k // nx * nx + (k + d) % nx) for k in range(nx * ny)])

    def along_y(array, d):
        return lax.ppermute(array, "corpus", [(k, (k + nx * d) % (nx * ny)) for k in range(nx * ny)])

    q_other = other_core(queries)
    cot_other = other_core(cotangent)
    pairs = rows * count
    whole = lambda *dims: pl.BlockSpec(dims, lambda i, c: (0,) * len(dims))
    in_hbm = pl.BlockSpec(memory_space=pltpu.HBM)
    split = lambda a: a.reshape(nz, 2, owned, width)
    points = pl.pallas_call(
        augment,
        name="augment",
        out_shape=kept(count, 2 * WIDE, dtype=BF16),
        in_specs=[pl.BlockSpec(memory_space=pltpu.SMEM), in_hbm, in_hbm],
        out_specs=vmem(),
        scratch_shapes=[pltpu.VMEM((nz, owned, width), BF16)] * 2 + [pltpu.SemaphoreType.DMA((2, nz))],
        compiler_params=pltpu.CompilerParams(vmem_limit_bytes=VMEM_BYTES),
    )(place, *(pltpu.with_memory_space_constraint(split(a), pltpu.HBM) for a in (corpus, targets)))
    stats, kernel, caug_f, sumk = call(
        functools.partial(forward, scale),
        "forward",
        [shape(4, rows), kept(2 * rows, count, dtype=BF16), kept(2 * rows, WIDE, dtype=BF16), kept(2 * rows, LANES)],
        5,
        2 * pairs,
        2,
        [pltpu.VMEM((2 * rows, WIDE), BF16)],
    )(queries, q_other, cotangent, cot_other, in_vmem(points))

    points, kernel, caug_f, sumk = (in_vmem(a) for a in (points, kernel, caug_f, sumk))
    query_terms = lambda half, after: call(functools.partial(scored, half), "scored", shape(rows, LANES), 3, pairs, 2, unread=1)(
        caug_f, points, kernel, after
    )
    stats = stats + jnp.roll(other_core(stats), 2, axis=0)
    sums1 = query_terms(1, stats)
    stats = ring_sum(stats, along_x, nx)
    sums0 = query_terms(0, stats)
    arrived = [stats] + [along_y(stats, d) for d in range(1, ny)]
    both, g0, g1 = call(
        functools.partial(prepare, scale, beta),
        "prepare",
        [kept(2 * rows, 2 * WIDE, dtype=BF16), kept(rows, LANES), kept(rows, LANES)],
        10,
        rows,
        1,
    )(*arrived, queries, q_other, caug_f, sumk, sums0, sums1)
    both = in_vmem(both)

    g = (g0 + other_core(g1)).astype(BF16)
    gx = ring_sum(g, along_x, nx).astype(BF16)
    grad_query = ring_sum(gx, along_y, ny)

    def slice_of(d, after):
        piece = pl.BlockSpec((owned, 2 * WIDE), lambda i, c: (lax.rem(lax.div(c[0], 2) + d, nz), 0))
        outs = [shape(owned, WIDE, dtype=BF16)] if d else [shape(owned, LANES), shape(owned, LANES)]
        return pl.pallas_call(
            functools.partial(backward, scale, beta),
            name="backward",
            out_shape=outs,
            grid_spec=pltpu.PrefetchScalarGridSpec(
                num_scalar_prefetch=1,
                grid=(1,),
                in_specs=[piece, whole(2 * rows, 2 * WIDE), pl.BlockSpec(memory_space=pl.ANY)],
                out_specs=[whole(*o.shape) for o in outs],
            ),
            cost_estimate=cost(1, 4),
            compiler_params=pltpu.CompilerParams(vmem_limit_bytes=VMEM_BYTES),
        )(place, points, both, after)

    order = sorted(range(1, nz), key=lambda d: -min(d, nz - d))
    sent = [along_z(slice_of(d, after)[0], d) for d, after in zip(order, (g0, g, g))]
    own = slice_of(0, gx)
    for piece in sent:
        own = lax.optimization_barrier((own[0] + piece[:, :LANES].astype(F32), own[1] + piece[:, LANES:].astype(F32)))
    gy, gz = own
    return grad_query, gy, gz


def solution(mesh):
    nx = ny = math.isqrt(mesh.shape["corpus"])
    nz = mesh.shape["query"] // 2
    placed = (P("query", None), P("corpus", None), P("corpus", None), P("query", None))
    return jax.shard_map(
        functools.partial(body, nx, ny, nz),
        mesh=mesh,
        in_specs=placed,
        out_specs=(P("query", None), P(("corpus", "query"), None), P(("corpus", "query"), None)),
        check_vma=False,
    )
```

```python
import functools
import math

import jax
import jax.numpy as jnp
from jax import lax
from jax.experimental import pallas as pl
from jax.experimental.pallas import tpu as pltpu
from jax.sharding import PartitionSpec as P

F32, BF16 = jnp.float32, jnp.bfloat16
LANES = 128
WIDE = 2 * LANES
TILE = 512
SHORT, LONG = 256, 1024
VMEM_BYTES = 8 * 1024 * 1024
NT = (((1,), (1,)), ((), ()))
NN = (((1,), (0,)), ((), ()))


def dot(left, right, dims=NN):
    return lax.dot_general(left, right, dims, preferred_element_type=F32)


def split3(value):
    high = value.astype(BF16).astype(F32)
    rest = value - high
    mid = rest.astype(BF16).astype(F32)
    return high, mid, (rest - mid).astype(BF16).astype(F32)


def columns_tail(rows, entries):
    lane = lax.broadcasted_iota(jnp.int32, (rows, LANES), 1)
    tail = jnp.zeros((rows, LANES), F32)
    for k, entry in enumerate(entries):
        tail = jnp.where(lane == k, entry, tail)
    return tail.astype(BF16)


def row_sums(array):
    return jnp.sum(array.T, axis=0, keepdims=True)


def halves(ref):
    return ref.at[:, :WIDE], ref.at[:, WIDE:]


def augment(place_ref, y_hbm, z_hbm, points_ref, y, z, sems):
    yaug_ref, zaug_ref = halves(points_ref)
    core = lax.rem(place_ref[0], 2)
    slices, step = y.shape[:2]
    copies = [[pltpu.make_async_copy(h.at[s, core], v.at[s], sems.at[k, s]) for k, (h, v) in enumerate(((y_hbm, y), (z_hbm, z)))] for s in range(slices)]
    for pair in copies:
        for copy in pair:
            copy.start()
    zaug_ref[:, LANES:] = columns_tail(slices * step, [1.0, 1.0, 1.0])
    for s in range(slices):
        at = slice(s * step, (s + 1) * step)
        copies[s][0].wait()
        points = y[s]
        half = 0.5 * jnp.sum(jnp.square(points.astype(F32)), axis=1, keepdims=True)
        yaug_ref[at, :LANES] = points
        yaug_ref[at, LANES:] = columns_tail(step, [*split3(half), 1.0, 1.0, 1.0])
    for s in range(slices):
        copies[s][1].wait()
        zaug_ref[s * step : (s + 1) * step, :LANES] = z[s]


def forward(scale, q0_ref, q1_ref, c0_ref, c1_ref, points_ref, stats_ref, kernel_ref, caug_ref, sumk_ref, qaug):
    yaug_ref, zaug_ref = halves(points_ref)
    rows, count = q0_ref.shape[0], points_ref.shape[0]
    qaug[:, LANES:] = columns_tail(2 * rows, [-1.0, -1.0, -1.0])
    for half, (q_ref, c_ref) in enumerate(((q0_ref, c0_ref), (q1_ref, c1_ref))):
        base = half * rows
        qaug[base : base + rows, :LANES] = q_ref[...]
        caug_ref[base : base + rows, :LANES] = c_ref[...]
        for i in range(rows // SHORT):
            at = slice(base + i * SHORT, base + (i + 1) * SHORT)
            q = qaug[at, :]
            total = jnp.zeros((SHORT, LANES), F32)
            acc = jnp.zeros((SHORT, WIDE), F32)
            for j in range(count // LONG):
                js = slice(j * LONG, (j + 1) * LONG)
                kernel = jnp.exp2(dot(q, yaug_ref[js, :], NT) * scale)
                for u in range(LONG // LANES):
                    total = total + kernel[:, u * LANES : (u + 1) * LANES]
                rounded = kernel.astype(BF16)
                kernel_ref[at, js] = rounded
                both = jnp.concatenate([yaug_ref[js, :LANES], zaug_ref[js, :LANES]], axis=1)
                acc = acc + dot(rounded, both)
            sumk_ref[at, :] = acc[:, :LANES]
            weighted = c_ref[i * SHORT : (i + 1) * SHORT, :].astype(F32) * acc[:, LANES:]
            center = jnp.sum(weighted, axis=1, keepdims=True) / jnp.sum(total, axis=1, keepdims=True)
            caug_ref[at, LANES:] = columns_tail(SHORT, [-t for t in split3(center)])
            cols = slice(i * SHORT, (i + 1) * SHORT)
            stats_ref[2 * half : 2 * half + 1, cols] = row_sums(total)
            stats_ref[2 * half + 1 : 2 * half + 2, cols] = row_sums(weighted)


def scored(half, caug_ref, points_ref, kernel_ref, _, out_ref):
    yaug_ref, zaug_ref = halves(points_ref)
    rows, count = out_ref.shape[0], points_ref.shape[0]
    for i in range(rows // SHORT):
        at = slice(half * rows + i * SHORT, half * rows + (i + 1) * SHORT)
        cot = caug_ref[at, :]
        acc = jnp.zeros((SHORT, LANES), F32)
        for j in range(count // LONG):
            js = slice(j * LONG, (j + 1) * LONG)
            score = dot(cot, zaug_ref[js, :], NT)
            weighted = kernel_ref[at, js].astype(F32) * score
            acc = acc + dot(weighted.astype(BF16), yaug_ref[js, :LANES])
        out_ref[i * SHORT : (i + 1) * SHORT, :] = acc


def prepare(scale, beta, s0, s1, s2, s3, q0, q1, caug_f, sumk, sums0, sums1, both_ref, g0, g1):
    qaug_ref, caug_ref = halves(both_ref)
    stats = (s0[...] + s2[...]) + (s1[...] + s3[...])
    rows = q0.shape[0]
    row = lax.broadcasted_iota(jnp.int32, (LANES, rows), 0)
    for k, (q, sums, g) in enumerate(((q0, sums0, g0), (q1, sums1, g1))):
        total = stats[2 * k : 2 * k + 1, :]
        recip = 1.0 / total
        inner = stats[2 * k + 1 : 2 * k + 2, :] * recip
        lift = jnp.log2(total) * (-1.0 / scale)
        half = LANES // 2
        tails = jnp.where(row < 3, -1.0, jnp.where(row == half + 3, recip * beta, jnp.zeros((LANES, rows), F32)))
        for n, (a, b) in enumerate(zip(split3(lift), split3(inner))):
            tails = jnp.where(row == 3 + n, a, tails)
            tails = jnp.where(row == half + n, -b, tails)
        tails = tails.T
        at = slice(k * rows, (k + 1) * rows)
        ct = pltpu.roll(tails, half, 1)
        lane = lax.broadcasted_iota(jnp.int32, (rows, LANES), 1)
        qaug_ref[at, :LANES] = q[...]
        qaug_ref[at, LANES:] = jnp.where(lane < 6, tails, 0.0).astype(BF16)
        caug_ref[at, :LANES] = caug_f[at, :LANES]
        caug_ref[at, LANES:] = jnp.where(lane < 3, ct, 0.0).astype(BF16)
        center = -jnp.sum(caug_f[at, LANES:].astype(F32), axis=1, keepdims=True)
        shift = jnp.sum(jnp.where(lane < 3, ct, 0.0), axis=1, keepdims=True) + center
        g[...] = ct[:, 3:4] * (sums[...] + shift * sumk[at, :])


def backward(scale, beta, at_ref, points_ref, both_ref, _, *out_refs):
    (yaug_ref, zaug_ref), (qaug_ref, caug_ref) = halves(points_ref), halves(both_ref)
    step, rows = points_ref.shape[0], both_ref.shape[0]
    for j in range(step // TILE):
        js = slice(j * TILE, (j + 1) * TILE)
        yaug, zaug = yaug_ref[js, :], zaug_ref[js, :]
        gy = jnp.zeros((TILE, WIDE), F32)
        gz = jnp.zeros((TILE, LANES), F32)
        for i in range(rows // TILE):
            at = slice(i * TILE, (i + 1) * TILE)
            q, cot = qaug_ref[at, :], caug_ref[at, :]
            prob = jnp.exp2(dot(yaug, q, NT) * scale)
            adjoint = prob * dot(zaug, cot, NT)
            gy = gy + dot(adjoint.astype(BF16), q)
            gz = gz + dot(prob.astype(BF16), cot[:, :LANES])
        gy = beta * (gy[:, :LANES] + gy[:, LANES : LANES + 1] * yaug[:, :LANES].astype(F32))
        if len(out_refs) == 1:
            out_refs[0][js, :LANES] = gy.astype(BF16)
            out_refs[0][js, LANES:] = gz.astype(BF16)
        else:
            out_refs[0][js, :] = gy
            out_refs[1][js, :] = gz


def shape(*dims, dtype=F32):
    return jax.ShapeDtypeStruct(dims, dtype)


def kept(*dims, dtype=F32):
    return pltpu.VMEM(dims, dtype)


def vmem():
    return pl.BlockSpec(memory_space=pltpu.VMEM)


def cost(pairs, units):
    return pl.CostEstimate(flops=units * 2 * pairs * WIDE, bytes_accessed=1 << 16, transcendentals=0)


def call(body, name, outs, n_in, pairs, units, scratch=(), unread=0):
    return pl.pallas_call(
        body,
        name=name,
        out_shape=outs,
        in_specs=[vmem()] * n_in + [pl.BlockSpec(memory_space=pl.ANY)] * unread,
        out_specs=jax.tree.map(lambda _: vmem(), outs),
        scratch_shapes=list(scratch),
        cost_estimate=cost(pairs, units),
        compiler_params=pltpu.CompilerParams(vmem_limit_bytes=VMEM_BYTES),
    )


def in_vmem(array):
    return pltpu.with_memory_space_constraint(array, pltpu.VMEM)


def ring_sum(array, along, n):
    parts = [array] + [along(array, d) for d in range(1, n)]
    return (parts[0].astype(F32) + parts[2].astype(F32)) + (parts[1].astype(F32) + parts[3].astype(F32))


def body(nx, ny, nz, queries, corpus, targets, cotangent):
    rows, width = queries.shape
    owned = corpus.shape[0] // (2 * nz)
    count = nz * owned
    beta = 4.5 / math.sqrt(width)
    scale = beta * math.log2(math.e)
    place = lax.axis_index("query").astype(jnp.int32)[None]
    swap = [(k, k ^ 1) for k in range(2 * nz)]

    def other_core(array):
        return lax.ppermute(array, "query", swap)

    def along_z(array, d):
        return lax.ppermute(array, "query", [(k, (k + 2 * d) % (2 * nz)) for k in range(2 * nz)])

    def along_x(array, d):
        return lax.ppermute(array, "corpus", [(k, k // nx * nx + (k + d) % nx) for k in range(nx * ny)])

    def along_y(array, d):
        return lax.ppermute(array, "corpus", [(k, (k + nx * d) % (nx * ny)) for k in range(nx * ny)])

    q_other = other_core(queries)
    cot_other = other_core(cotangent)
    pairs = rows * count
    whole = lambda *dims: pl.BlockSpec(dims, lambda i, c: (0,) * len(dims))
    in_hbm = pl.BlockSpec(memory_space=pltpu.HBM)
    split = lambda a: a.reshape(nz, 2, owned, width)
    points = pl.pallas_call(
        augment,
        name="augment",
        out_shape=kept(count, 2 * WIDE, dtype=BF16),
        in_specs=[pl.BlockSpec(memory_space=pltpu.SMEM), in_hbm, in_hbm],
        out_specs=vmem(),
        scratch_shapes=[pltpu.VMEM((nz, owned, width), BF16)] * 2 + [pltpu.SemaphoreType.DMA((2, nz))],
        compiler_params=pltpu.CompilerParams(vmem_limit_bytes=VMEM_BYTES),
    )(place, *(pltpu.with_memory_space_constraint(split(a), pltpu.HBM) for a in (corpus, targets)))
    stats, kernel, caug_f, sumk = call(
        functools.partial(forward, scale),
        "forward",
        [shape(4, rows), kept(2 * rows, count, dtype=BF16), kept(2 * rows, WIDE, dtype=BF16), kept(2 * rows, LANES)],
        5,
        2 * pairs,
        2,
        [pltpu.VMEM((2 * rows, WIDE), BF16)],
    )(queries, q_other, cotangent, cot_other, in_vmem(points))

    points, kernel, caug_f, sumk = (in_vmem(a) for a in (points, kernel, caug_f, sumk))
    query_terms = lambda half, after: call(functools.partial(scored, half), "scored", shape(rows, LANES), 3, pairs, 2, unread=1)(
        caug_f, points, kernel, after
    )
    stats = stats + jnp.roll(other_core(stats), 2, axis=0)
    sums1 = query_terms(1, stats)
    stats = ring_sum(stats, along_x, nx)
    sums0 = query_terms(0, stats)
    arrived = [stats] + [along_y(stats, d) for d in range(1, ny)]
    both, g0, g1 = call(
        functools.partial(prepare, scale, beta),
        "prepare",
        [kept(2 * rows, 2 * WIDE, dtype=BF16), kept(rows, LANES), kept(rows, LANES)],
        10,
        rows,
        1,
    )(*arrived, queries, q_other, caug_f, sumk, sums0, sums1)
    both = in_vmem(both)

    g = (g0 + other_core(g1)).astype(BF16)
    gx = ring_sum(g, along_x, nx).astype(BF16)
    grad_query = ring_sum(gx, along_y, ny)

    def slice_of(d, after):
        piece = pl.BlockSpec((owned, 2 * WIDE), lambda i, c: (lax.rem(lax.div(c[0], 2) + d, nz), 0))
        outs = [shape(owned, WIDE, dtype=BF16)] if d else [shape(owned, LANES), shape(owned, LANES)]
        return pl.pallas_call(
            functools.partial(backward, scale, beta),
            name="backward",
            out_shape=outs,
            grid_spec=pltpu.PrefetchScalarGridSpec(
                num_scalar_prefetch=1,
                grid=(1,),
                in_specs=[piece, whole(2 * rows, 2 * WIDE), pl.BlockSpec(memory_space=pl.ANY)],
                out_specs=[whole(*o.shape) for o in outs],
            ),
            cost_estimate=cost(1, 4),
            compiler_params=pltpu.CompilerParams(vmem_limit_bytes=VMEM_BYTES),
        )(place, points, both, after)

    order = sorted(range(1, nz), key=lambda d: -min(d, nz - d))
    sent = [along_z(slice_of(d, after)[0], d) for d, after in zip(order, (g0, g, g))]
    own = slice_of(0, gx)
    for piece in sent:
        own = lax.optimization_barrier((own[0] + piece[:, :LANES].astype(F32), own[1] + piece[:, LANES:].astype(F32)))
    gy, gz = own
    return grad_query, gy, gz


def solution(mesh):
    nx = ny = math.isqrt(mesh.shape["corpus"])
    nz = mesh.shape["query"] // 2
    placed = (P("query", None), P("corpus", None), P("corpus", None), P("query", None))
    return jax.shard_map(
        functools.partial(body, nx, ny, nz),
        mesh=mesh,
        in_specs=placed,
        out_specs=(P("query", None), P(("corpus", "query"), None), P(("corpus", "query"), None)),
        check_vma=False,
    )
```

```python
import functools
import math

import jax
import jax.numpy as jnp
from jax import lax
from jax.experimental import pallas as pl
from jax.experimental.pallas import tpu as pltpu
from jax.sharding import PartitionSpec as P

F32, BF16 = jnp.float32, jnp.bfloat16
LANES = 128
WIDE = 2 * LANES
TALL, TILE = 1024, 512
SHORT, LONG = 256, 1024
VMEM_BYTES = 12 * 1024 * 1024
NT = (((1,), (1,)), ((), ()))
NN = (((1,), (0,)), ((), ()))


def dot(left, right, dims=NN):
    return lax.dot_general(left, right, dims, preferred_element_type=F32)


def split3(value):
    high = value.astype(BF16).astype(F32)
    rest = value - high
    mid = rest.astype(BF16).astype(F32)
    return high, mid, (rest - mid).astype(BF16).astype(F32)


def columns_tail(rows, entries):
    lane = lax.broadcasted_iota(jnp.int32, (rows, LANES), 1)
    tail = jnp.zeros((rows, LANES), F32)
    for k, entry in enumerate(entries):
        tail = jnp.where(lane == k, entry, tail)
    return tail.astype(BF16)


def row_sums(array):
    return jnp.sum(array.T, axis=0, keepdims=True)


def halves(ref):
    return ref.at[:, :WIDE], ref.at[:, WIDE:]


def augment(place_ref, y_hbm, z_hbm, points_ref, y, z, sems):
    yaug_ref, zaug_ref = halves(points_ref)
    core = lax.rem(place_ref[0], 2)
    slices, step = y.shape[:2]
    copies = [[pltpu.make_async_copy(h.at[s, core], v.at[s], sems.at[k, s]) for k, (h, v) in enumerate(((y_hbm, y), (z_hbm, z)))] for s in range(slices)]
    for pair in copies:
        for copy in pair:
            copy.start()
    zaug_ref[:, LANES:] = columns_tail(slices * step, [1.0, 1.0, 1.0])
    for s in range(slices):
        at = slice(s * step, (s + 1) * step)
        copies[s][0].wait()
        points = y[s]
        half = 0.5 * jnp.sum(jnp.square(points.astype(F32)), axis=1, keepdims=True)
        yaug_ref[at, :LANES] = points
        yaug_ref[at, LANES:] = columns_tail(step, [*split3(half), 1.0, 1.0, 1.0])
    for s in range(slices):
        copies[s][1].wait()
        zaug_ref[s * step : (s + 1) * step, :LANES] = z[s]


def forward(scale, q0_ref, q1_ref, c0_ref, c1_ref, points_ref, stats_ref, kernel_ref, caug_ref, sumk_ref, qaug):
    yaug_ref, zaug_ref = halves(points_ref)
    rows, count = q0_ref.shape[0], points_ref.shape[0]
    qaug[:, LANES:] = columns_tail(2 * rows, [-1.0, -1.0, -1.0])
    for half, (q_ref, c_ref) in enumerate(((q0_ref, c0_ref), (q1_ref, c1_ref))):
        base = half * rows
        qaug[base : base + rows, :LANES] = q_ref[...]
        caug_ref[base : base + rows, :LANES] = c_ref[...]
        for i in range(rows // SHORT):
            at = slice(base + i * SHORT, base + (i + 1) * SHORT)
            q = qaug[at, :]
            total = jnp.zeros((SHORT, LANES), F32)
            acc = jnp.zeros((SHORT, WIDE), F32)
            for j in range(count // LONG):
                js = slice(j * LONG, (j + 1) * LONG)
                kernel = jnp.exp2(dot(q, yaug_ref[js, :], NT) * scale)
                for u in range(LONG // LANES):
                    total = total + kernel[:, u * LANES : (u + 1) * LANES]
                rounded = kernel.astype(BF16)
                kernel_ref[at, js] = rounded
                both = jnp.concatenate([yaug_ref[js, :LANES], zaug_ref[js, :LANES]], axis=1)
                acc = acc + dot(rounded, both)
            sumk_ref[at, :] = acc[:, :LANES]
            weighted = c_ref[i * SHORT : (i + 1) * SHORT, :].astype(F32) * acc[:, LANES:]
            center = jnp.sum(weighted, axis=1, keepdims=True) / jnp.sum(total, axis=1, keepdims=True)
            caug_ref[at, LANES:] = columns_tail(SHORT, [-t for t in split3(center)])
            cols = slice(i * SHORT, (i + 1) * SHORT)
            stats_ref[2 * half : 2 * half + 1, cols] = row_sums(total)
            stats_ref[2 * half + 1 : 2 * half + 2, cols] = row_sums(weighted)


def scored(half, caug_ref, points_ref, kernel_ref, _, out_ref):
    yaug_ref, zaug_ref = halves(points_ref)
    rows, count = out_ref.shape[0], points_ref.shape[0]
    for i in range(rows // SHORT):
        at = slice(half * rows + i * SHORT, half * rows + (i + 1) * SHORT)
        cot = caug_ref[at, :]
        acc = jnp.zeros((SHORT, LANES), F32)
        for j in range(count // LONG):
            js = slice(j * LONG, (j + 1) * LONG)
            score = dot(cot, zaug_ref[js, :], NT)
            weighted = kernel_ref[at, js].astype(F32) * score
            acc = acc + dot(weighted.astype(BF16), yaug_ref[js, :LANES])
        out_ref[i * SHORT : (i + 1) * SHORT, :] = acc


def prepare(scale, beta, s0, s1, s2, s3, q0, q1, caug_f, sumk, sums0, sums1, both_ref, g0, g1):
    qaug_ref, caug_ref = halves(both_ref)
    stats = (s0[...] + s2[...]) + (s1[...] + s3[...])
    rows = q0.shape[0]
    row = lax.broadcasted_iota(jnp.int32, (LANES, rows), 0)
    for k, (q, sums, g) in enumerate(((q0, sums0, g0), (q1, sums1, g1))):
        total = stats[2 * k : 2 * k + 1, :]
        recip = 1.0 / total
        inner = stats[2 * k + 1 : 2 * k + 2, :] * recip
        lift = jnp.log2(total) * (-1.0 / scale)
        half = LANES // 2
        tails = jnp.where(row < 3, -1.0, jnp.where(row == half + 3, recip * beta, jnp.zeros((LANES, rows), F32)))
        for n, (a, b) in enumerate(zip(split3(lift), split3(inner))):
            tails = jnp.where(row == 3 + n, a, tails)
            tails = jnp.where(row == half + n, -b, tails)
        tails = tails.T
        at = slice(k * rows, (k + 1) * rows)
        ct = pltpu.roll(tails, half, 1)
        lane = lax.broadcasted_iota(jnp.int32, (rows, LANES), 1)
        qaug_ref[at, :LANES] = q[...]
        qaug_ref[at, LANES:] = jnp.where(lane < 6, tails, 0.0).astype(BF16)
        caug_ref[at, :LANES] = caug_f[at, :LANES]
        caug_ref[at, LANES:] = jnp.where(lane < 3, ct, 0.0).astype(BF16)
        center = -jnp.sum(caug_f[at, LANES:].astype(F32), axis=1, keepdims=True)
        shift = jnp.sum(jnp.where(lane < 3, ct, 0.0), axis=1, keepdims=True) + center
        g[...] = ct[:, 3:4] * (sums[...] + shift * sumk[at, :])


def backward(scale, beta, at_ref, points_ref, both_ref, _, *out_refs):
    (yaug_ref, zaug_ref), (qaug_ref, caug_ref) = halves(points_ref), halves(both_ref)
    step, rows = points_ref.shape[0], both_ref.shape[0]
    for j in range(step // TALL):
        js = slice(j * TALL, (j + 1) * TALL)
        yaug, zaug = yaug_ref[js, :], zaug_ref[js, :]
        gy = jnp.zeros((TALL, WIDE), F32)
        gz = jnp.zeros((TALL, LANES), F32)
        for i in range(rows // TILE):
            at = slice(i * TILE, (i + 1) * TILE)
            q, cot = qaug_ref[at, :], caug_ref[at, :]
            prob = jnp.exp2(dot(yaug, q, NT) * scale)
            adjoint = prob * dot(zaug, cot, NT)
            gy = gy + dot(adjoint.astype(BF16), q)
            gz = gz + dot(prob.astype(BF16), cot[:, :LANES])
        gy = beta * (gy[:, :LANES] + gy[:, LANES : LANES + 1] * yaug[:, :LANES].astype(F32))
        if len(out_refs) == 1:
            out_refs[0][js, :LANES] = gy.astype(BF16)
            out_refs[0][js, LANES:] = gz.astype(BF16)
        else:
            out_refs[0][js, :] = gy
            out_refs[1][js, :] = gz


def shape(*dims, dtype=F32):
    return jax.ShapeDtypeStruct(dims, dtype)


def kept(*dims, dtype=F32):
    return pltpu.VMEM(dims, dtype)


def vmem():
    return pl.BlockSpec(memory_space=pltpu.VMEM)


def cost(pairs, units):
    return pl.CostEstimate(flops=units * 2 * pairs * WIDE, bytes_accessed=1 << 16, transcendentals=0)


def call(body, name, outs, n_in, pairs, units, scratch=(), unread=0):
    return pl.pallas_call(
        body,
        name=name,
        out_shape=outs,
        in_specs=[vmem()] * n_in + [pl.BlockSpec(memory_space=pl.ANY)] * unread,
        out_specs=jax.tree.map(lambda _: vmem(), outs),
        scratch_shapes=list(scratch),
        cost_estimate=cost(pairs, units),
        compiler_params=pltpu.CompilerParams(vmem_limit_bytes=VMEM_BYTES),
    )


def in_vmem(array):
    return pltpu.with_memory_space_constraint(array, pltpu.VMEM)


def ring_sum(array, along, n):
    parts = [array] + [along(array, d) for d in range(1, n)]
    return (parts[0].astype(F32) + parts[2].astype(F32)) + (parts[1].astype(F32) + parts[3].astype(F32))


def body(nx, ny, nz, queries, corpus, targets, cotangent):
    rows, width = queries.shape
    owned = corpus.shape[0] // (2 * nz)
    count = nz * owned
    beta = 4.5 / math.sqrt(width)
    scale = beta * math.log2(math.e)
    place = lax.axis_index("query").astype(jnp.int32)[None]
    swap = [(k, k ^ 1) for k in range(2 * nz)]

    def other_core(array):
        return lax.ppermute(array, "query", swap)

    def along_z(array, d):
        return lax.ppermute(array, "query", [(k, (k + 2 * d) % (2 * nz)) for k in range(2 * nz)])

    def along_x(array, d):
        return lax.ppermute(array, "corpus", [(k, k // nx * nx + (k + d) % nx) for k in range(nx * ny)])

    def along_y(array, d):
        return lax.ppermute(array, "corpus", [(k, (k + nx * d) % (nx * ny)) for k in range(nx * ny)])

    q_other = other_core(queries)
    cot_other = other_core(cotangent)
    pairs = rows * count
    whole = lambda *dims: pl.BlockSpec(dims, lambda i, c: (0,) * len(dims))
    in_hbm = pl.BlockSpec(memory_space=pltpu.HBM)
    split = lambda a: a.reshape(nz, 2, owned, width)
    points = pl.pallas_call(
        augment,
        name="augment",
        out_shape=kept(count, 2 * WIDE, dtype=BF16),
        in_specs=[pl.BlockSpec(memory_space=pltpu.SMEM), in_hbm, in_hbm],
        out_specs=vmem(),
        scratch_shapes=[pltpu.VMEM((nz, owned, width), BF16)] * 2 + [pltpu.SemaphoreType.DMA((2, nz))],
        compiler_params=pltpu.CompilerParams(vmem_limit_bytes=VMEM_BYTES),
    )(place, *(pltpu.with_memory_space_constraint(split(a), pltpu.HBM) for a in (corpus, targets)))
    stats, kernel, caug_f, sumk = call(
        functools.partial(forward, scale),
        "forward",
        [shape(4, rows), kept(2 * rows, count, dtype=BF16), kept(2 * rows, WIDE, dtype=BF16), kept(2 * rows, LANES)],
        5,
        2 * pairs,
        2,
        [pltpu.VMEM((2 * rows, WIDE), BF16)],
    )(queries, q_other, cotangent, cot_other, in_vmem(points))

    points, kernel, caug_f, sumk = (in_vmem(a) for a in (points, kernel, caug_f, sumk))
    query_terms = lambda half, after: call(functools.partial(scored, half), "scored", shape(rows, LANES), 3, pairs, 2, unread=1)(
        caug_f, points, kernel, after
    )
    stats = stats + jnp.roll(other_core(stats), 2, axis=0)
    sums1 = query_terms(1, stats)
    stats = ring_sum(stats, along_x, nx)
    sums0 = query_terms(0, stats)
    arrived = [stats] + [along_y(stats, d) for d in range(1, ny)]
    both, g0, g1 = call(
        functools.partial(prepare, scale, beta),
        "prepare",
        [kept(2 * rows, 2 * WIDE, dtype=BF16), kept(rows, LANES), kept(rows, LANES)],
        10,
        rows,
        1,
    )(*arrived, queries, q_other, caug_f, sumk, sums0, sums1)
    both = in_vmem(both)

    g = (g0 + other_core(g1)).astype(BF16)
    gx = ring_sum(g, along_x, nx).astype(BF16)
    grad_query = ring_sum(gx, along_y, ny)

    def slice_of(d, after):
        piece = pl.BlockSpec((owned, 2 * WIDE), lambda i, c: (lax.rem(lax.div(c[0], 2) + d, nz), 0))
        outs = [shape(owned, WIDE, dtype=BF16)] if d else [shape(owned, LANES), shape(owned, LANES)]
        return pl.pallas_call(
            functools.partial(backward, scale, beta),
            name="backward",
            out_shape=outs,
            grid_spec=pltpu.PrefetchScalarGridSpec(
                num_scalar_prefetch=1,
                grid=(1,),
                in_specs=[piece, whole(2 * rows, 2 * WIDE), pl.BlockSpec(memory_space=pl.ANY)],
                out_specs=[whole(*o.shape) for o in outs],
            ),
            cost_estimate=cost(1, 4),
            compiler_params=pltpu.CompilerParams(vmem_limit_bytes=VMEM_BYTES),
        )(place, points, both, after)

    order = sorted(range(1, nz), key=lambda d: -min(d, nz - d))
    sent = [along_z(slice_of(d, after)[0], d) for d, after in zip(order, (g0, g, g))]
    own = slice_of(0, gx)
    for piece in sent:
        own = lax.optimization_barrier((own[0] + piece[:, :LANES].astype(F32), own[1] + piece[:, LANES:].astype(F32)))
    gy, gz = own
    return grad_query, gy, gz


def solution(mesh):
    nx = ny = math.isqrt(mesh.shape["corpus"])
    nz = mesh.shape["query"] // 2
    placed = (P("query", None), P("corpus", None), P("corpus", None), P("query", None))
    return jax.shard_map(
        functools.partial(body, nx, ny, nz),
        mesh=mesh,
        in_specs=placed,
        out_specs=(P("query", None), P(("corpus", "query"), None), P(("corpus", "query"), None)),
        check_vma=False,
    )
```
